256 devices in a mesh: row: 32 (over y, z), col: 8 (over x, core).
Axes of the slice: x: 4, y: 4, z: 8, core: 2. Of those that a mesh axis runs over, the one named last changes fastest.
Arguments:
- acts: bfloat16 [65536, 4096], P('row', 'col'), may hold values from -6 to 6
- out_grads: bfloat16 [65536, 1, 4096], P('row', None, 'col'), may hold values from -0.01171875 to 0.01171875
- row_stat: float32 [1, 4096], P(None, 'row'), may hold values from 0.02 to 0.2
- col_stat: float32 [1, 4096], P(None, 'col'), may hold values from 0.02 to 0.2
- master: float32 [4096, 1, 4096], P('row', None, 'col'), may hold values from -0.09375 to 0.09375
Outputs:
- fresh_weights: bfloat16 [4096, 1, 4096], P(None, None, 'col')
- master_out: float32 [4096, 1, 4096], P('row', None, 'col')
- update_out: float32 [4096, 1, 4096], P('row', None, 'col')
- row_out: float32 [1, 4096], P(None, 'row')
- col_out: float32 [1, 4096], P(None, 'col')
The draws below stay inside these ranges and needn't reach their ends.
All inputs are finite; a program needn't handle non-finite values.
Results may differ from the reference program's by a relative error of at most 0.001.
Values may be sent and summed in bfloat16 or wider, within the bound.
No kernel may reach another device: no remote copies, remote signals or barrier semaphores. Data moves between devices by JAX's collectives and lax.ppermute only.
A program may use at most 256 MiB of HBM per device.

```python
import math
import jax
import jax.numpy as jnp
from jax import lax

D = 4096
MATS = 1
TOKENS = 65536


def strengthened(drawn, stream_key, source, target, blocks, factor):
    owner, partner = [(jnp.arange(drawn.shape[dim]) // (drawn.shape[dim] // blocks)).reshape([-1 if axis == dim else 1 for axis in range(drawn.ndim)]) for dim in (source, target)]
    chosen = jax.random.permutation(stream_key, blocks)[partner]
    strong = (owner == chosen) | (owner == (partner + blocks // 2) % blocks)
    return jnp.where(strong, factor * drawn, drawn)


def levels(own_key, extent, cuts, low, high):
    def one(dim, blocks):
        steps = jax.random.uniform(jax.random.fold_in(jax.random.fold_in(own_key, 6), dim), (blocks,), jnp.float32, low / len(cuts), high / len(cuts))
        return jnp.repeat(jnp.exp(steps), extent[dim] // blocks).reshape((-1,) + (1,) * (len(extent) - dim - 1))

    level = one(*cuts[0])
    for cut in cuts[1:]:
        level = level * one(*cut)
    return level


def normal_values(own_key, dims, scale, bound, cuts=(), dtype=jnp.bfloat16):
    drawn = scale * jax.random.normal(own_key, dims, jnp.float32)
    if cuts:
        drawn = drawn * levels(own_key, dims, cuts, -0.22, 0.18)
    return jnp.clip(drawn, -bound, bound).astype(dtype)


def noise_with(stream_key, shape, spread, reach, cuts, heavy, kind=jnp.bfloat16):
    result = spread * jax.random.normal(stream_key, shape, jnp.float32)
    if cuts:
        result = result * levels(stream_key, shape, cuts, -0.22, 0.18)
    return jnp.clip(strengthened(result, jax.random.fold_in(stream_key, 3), *heavy), -reach, reach).astype(kind)


def setup_inputs(seed: int = 0) -> dict:
    key_list = jax.random.split(jax.random.key(seed), 6)
    return {
        "acts": noise_with(key_list[0], (TOKENS, D), 1.0, 6.0, ((0, 32), (1, 8)), (0, 1, 32, 2.75)),
        "out_grads": normal_values(key_list[1], (TOKENS, MATS, D), (0.5 / TOKENS ** 0.5), 0.01171875, ((0, 32), (2, 8))),
        "row_stat": jnp.clip(jnp.exp(math.log(0.2) - 2.3025851 * jax.random.uniform(key_list[2], (MATS, D), jnp.float32) ** levels(key_list[2], (MATS, D), ((1, 32),), -0.2, 0.2)), 0.02, 0.2),
        "col_stat": jnp.clip(jnp.exp(math.log(0.2) - 2.3025851 * jax.random.uniform(key_list[3], (MATS, D), jnp.float32) ** levels(key_list[3], (MATS, D), ((1, 8),), -0.2, 0.2)), 0.02, 0.2),
        "master": normal_values(key_list[4], (D, MATS, D), D ** -0.5, 0.09375, ((0, 32), (2, 8)), jnp.float32),
    }


def reference(acts, out_grads, row_stat, col_stat, master):
    flat = out_grads.reshape(TOKENS, MATS * D)
    grad = jnp.dot(acts.T, flat, preferred_element_type=jnp.float32).reshape(D, MATS, D)
    squares = grad * grad + 1e-30
    row_out = 0.75 * row_stat + 0.25 * lax.optimization_barrier(jnp.sum(squares, axis=2)).T / D
    col_out = 0.75 * col_stat + 0.25 * lax.optimization_barrier(jnp.sum(squares, axis=0)) / D
    row_mean = lax.optimization_barrier(jnp.sum(row_out, axis=1)) / D
    raw = grad * lax.rsqrt(row_out.T[:, :, None] * col_out[None, :, :] / row_mean[None, :, None])
    rms = jnp.sqrt(lax.optimization_barrier(jnp.sum(raw * raw, axis=(0, 2))) / (D * D))
    update_out = raw / jnp.maximum(1.0, rms)[None, :, None]
    master_out = master - 0.01 * update_out
    return (master_out.astype(jnp.bfloat16), master_out, update_out, row_out, col_out)
```

```python
import jax
import jax.numpy as jnp
from jax import lax
from jax.sharding import Mesh, PartitionSpec as P

D = 4096
SLICES = 4
Y_SCALE = 256.0
Z_SCALE = 64.0
F32 = jnp.float32


def ring(n, s):
    return [(i, (i + s) % n) for i in range(n)]


def contract_tokens(left, right):
    return lax.dot_general(
        left, right, (((0,), (0,)), ((), ())), preferred_element_type=F32
    )


def gather_z(part):
    up, down = [part], [part]
    for step in range(4):
        up.append(lax.ppermute(up[-1], "z", ring(8, 1)))
        if step < 3:
            down.append(lax.ppermute(down[-1], "z", ring(8, -1)))
    return jnp.stack([part, down[1], down[2], down[3], up[4], up[3], up[2], up[1]])


def gather_y(part):
    half = part.shape[0] // 2
    below = lax.ppermute(part, "y", ring(4, 1))
    above = lax.ppermute(part, "y", ring(4, -1))
    far_a = lax.ppermute(below[:half], "y", ring(4, 1))
    far_b = lax.ppermute(above[half:], "y", ring(4, -1))
    return jnp.stack([part, above, jnp.concatenate([far_a, far_b]), below])


def in_order(blocks, first, axis):
    n = blocks.shape[axis]
    return lax.dynamic_slice_in_dim(jnp.concatenate([blocks, blocks], axis), lax.rem(n - first, n), n, axis)


def shards(acts, out_grads, row_stat, col_stat, master):
    y, z, x, c = (lax.axis_index(a) for a in ("y", "z", "x", "c"))
    swap = ring(2, 1)
    mine = out_grads.reshape(out_grads.shape[0], -1)
    tokens, width = mine.shape
    both = jnp.concatenate([mine, lax.ppermute(mine, "c", swap)], axis=1)
    feat = acts.shape[1] // SLICES
    near, far = [], []
    for k in range(SLICES):
        part = acts[:, k * feat:(k + 1) * feat]
        near.append((part, lax.ppermute(part, "x", ring(4, -1)), lax.ppermute(part, "x", ring(4, 1))))
    summed = []
    for k in range(SLICES):
        part, above, below = near[k]
        far = jnp.concatenate([
            lax.ppermute(below[:tokens // 2], "x", ring(4, 1)),
            lax.ppermute(above[tokens // 2:], "x", ring(4, -1)),
        ])
        partial = contract_tokens(jnp.concatenate([part, above, far, below], axis=1), both)
        partial = partial.reshape(4, feat, 2 * width)
        total = lax.dynamic_index_in_dim(partial, lax.rem(y - x + 4, 4), 0, keepdims=False)
        arrived = []
        for s in range(1, 4):
            piece = lax.dynamic_index_in_dim(partial, lax.rem(y + s - x + 4, 4), 0, keepdims=False)
            arrived.append(lax.ppermute((piece * Y_SCALE).astype(jnp.float16), "y", ring(4, s)))
        total = total + (arrived[0].astype(F32) + arrived[1].astype(F32) + arrived[2].astype(F32)) * (1.0 / Y_SCALE)
        summed.append((total[:, :width], lax.ppermute(total[:, width:], "c", swap)))
    kept = jnp.concatenate([s[0] for s in summed])
    given = jnp.concatenate([s[1] for s in summed])
    lower, upper = jnp.where(c == 0, kept, given), jnp.where(c == 0, given, kept)
    outgoing = (jnp.concatenate([lower, upper]) * Z_SCALE).astype(jnp.float16)
    incoming = lax.all_to_all(outgoing, "z", 0, 0, tiled=True)
    rows = master.shape[0]
    grad = jnp.sum(incoming.reshape(8, rows, width).astype(F32), axis=0) * (1.0 / Z_SCALE)

    squares = grad * grad + 1e-30
    row_part = jnp.sum(squares, axis=1).reshape(1, rows)
    col_part = jnp.sum(squares, axis=0).reshape(1, width)
    row_part = row_part + lax.ppermute(row_part, "c", swap)
    one, two, three = (lax.ppermute(row_part, "x", ring(4, s)) for s in (1, 2, 3))
    row_sum = (row_part + two) + (one + three)
    col_all = lax.all_to_all(jnp.broadcast_to(col_part, (32, width)), ("y", "z"), 0, 0, tiled=True)
    col_sum = jnp.sum(col_all, axis=0, keepdims=True)
    row_out = 0.75 * row_stat + 0.25 * row_sum / D
    col_out = 0.75 * col_stat + 0.25 * col_sum / D
    base = grad * lax.rsqrt(row_out.T * col_out)
    lane = lax.broadcasted_iota(jnp.int32, (256, 128), 1)
    sums = jnp.where(lane == 0, jnp.sum(base * base), jnp.where(lane == 1, jnp.sum(row_out) * 0.125, 0.0))
    sums = jnp.sum(lax.all_to_all(sums, ("y", "z", "x", "c"), 0, 0, tiled=True), axis=0)
    row_mean = sums[1] / D
    rms = jnp.sqrt(row_mean * sums[0] / (D * D))
    update_out = base * (jnp.sqrt(row_mean) / jnp.maximum(1.0, rms))
    master_out = master.reshape(rows, width) - 0.01 * update_out
    fresh = master_out.astype(jnp.bfloat16)

    half = width // 2
    left = gather_y(gather_z(fresh[:, :half]))
    right = jnp.swapaxes(gather_z(gather_y(fresh[:, half:])), 0, 1)
    whole = jnp.concatenate([left, right], axis=3)
    whole = in_order(in_order(whole, y, 0), z, 1)
    return (
        whole.reshape(D, 1, width),
        master_out.reshape(master.shape),
        update_out.reshape(master.shape),
        row_out,
        col_out,
    )


def solution(mesh):
    fine = Mesh(mesh.devices.reshape(4, 8, 4, 2), ("y", "z", "x", "c"))
    row, col = ("y", "z"), ("x", "c")
    in_specs = (P(row, col), P(row, None, col), P(None, row), P(None, col), P(row, None, col))
    out_specs = (P(None, None, col), P(row, None, col), P(row, None, col), P(None, row), P(None, col))
    return jax.shard_map(shards, mesh=fine, in_specs=in_specs, out_specs=out_specs, check_vma=False)
```
